512 devices in a mesh: rep: 32 (over z, x), tp: 16 (over y, core).
Axes of the slice: x: 4, y: 8, z: 8, core: 2. Of those that a mesh axis runs over, the one named last changes fastest.
Arguments:
- hidden: bfloat16 [32768, 8192], P('rep', 'tp'), may hold values from -6 to 6
- grad_out: bfloat16 [32768, 2048], P('rep'), may hold values from -6 to 6
- weight: bfloat16 [32, 8192, 2048], P('rep', 'tp'), may hold values from -0.125 to 0.125
- alive: int32 [32, 16], replicated, may hold values from 0 to 1, as said below
Outputs:
- grad_hidden: bfloat16 [32768, 8192], P('rep', 'tp')
- grad_weight: float32 [7168, 2048], P('tp', 'rep')
The draws below stay inside these ranges and needn't reach their ends.
Inputs may be any that keep to these rules, and one draw needn't show every extreme that they name: `alive`: exactly 8 replicas have exactly two zeros in their row; every other row is all ones.
All inputs are finite; a program needn't handle non-finite values.
Results may differ from the reference program's by a relative error of at most 0.001.
Values may be sent and summed in bfloat16 or wider, within the bound.
No kernel may reach another device: no remote copies, remote signals or barrier semaphores. Data moves between devices by JAX's collectives and lax.ppermute only.
A program may use at most 64 MiB of HBM per device.

```python
import jax
import jax.numpy as jnp
from jax import lax

D = 2048
FF = 7168
TOK = 1024
SLOT = 512
TOKENS = 32768
DEGRADED = 8
N_REP = 32
N_TP = 16


def draw_alive(key, part):
    key_rep = jax.random.fold_in(key, 11)
    key_dev = jax.random.fold_in(key, 23)
    order = jax.random.permutation(key_rep, N_REP)
    degraded = jnp.zeros((N_REP,), jnp.int32).at[order[:DEGRADED]].set(1)
    scores = jax.random.randint(key_dev, (N_REP, N_TP), 0, 1 << 20) * N_TP + jnp.arange(N_TP, dtype=jnp.int32)[None, :]
    ranks = jnp.argsort(jnp.argsort(scores, axis=1, stable=True), axis=1, stable=True)
    lost = (ranks < 2).astype(jnp.int32)
    return (1 - degraded[:, None] * lost).astype(jnp.int32)


def block_levels(stream_key, shape, split, low, high):
    factor_of, own = 1.0, jax.random.fold_in(stream_key, 6)
    for axis_at, shards_of in split:
        draws = jnp.exp(jax.random.uniform(jax.random.fold_in(own, axis_at), (shards_of,), jnp.float32, low / len(split), high / len(split)))
        factor_of = factor_of * jnp.repeat(draws, shape[axis_at] // shards_of).reshape([-1 if axis == axis_at else 1 for axis in range(len(shape))])
    return factor_of


def gaussian(stream_key, shape, scale, most, cuts=(), kind=jnp.bfloat16):
    drawn = scale * jax.random.normal(stream_key, shape, jnp.float32)
    if cuts:
        drawn = drawn * block_levels(stream_key, shape, cuts, -0.22, 0.18)
    return jnp.clip(drawn, -most, most).astype(kind)


def setup_inputs(seed: int = 0) -> dict:
    key_list = jax.random.split(jax.random.key(seed), 5)
    return {
        "hidden": gaussian(key_list[0], (TOKENS, N_TP * SLOT), 1.0, 6.0, ((0, 32), (1, 16))),
        "grad_out": gaussian(key_list[1], (TOKENS, D), 1.0, 6.0, ((0, 32),)),
        "weight": gaussian(key_list[2], (N_REP, N_TP * SLOT, D), D ** -0.5, 0.125, ((0, 32), (1, 16))),
        "alive": draw_alive(jax.random.fold_in(key_list[4], 71), 0),
    }


def reference(hidden, grad_out, weight, alive):
    def one_replica(carry_sum, replica):
        alive_row = alive[replica]
        live_count = jnp.sum(alive_row)
        slice_width = FF // live_count
        inclusive = jnp.cumsum(alive_row)
        tok_rows = lax.dynamic_slice_in_dim(grad_out, (replica * TOK).astype(jnp.int32), TOK, 0)
        hid_rows = lax.dynamic_slice_in_dim(hidden, (replica * TOK).astype(jnp.int32), TOK, 0)
        weights = weight[replica]
        columns = jnp.arange(N_TP * SLOT, dtype=jnp.int32)
        device_of = columns // SLOT
        within = columns % SLOT
        usable = (alive_row[device_of] == 1) & (within < slice_width)
        product = lax.dot_general(tok_rows, weights, (((1,), (1,)), ((), ())), preferred_element_type=jnp.float32)
        grad_rows = jnp.where(usable[None, :], product, 0.0).astype(jnp.bfloat16)
        units = jnp.arange(FF, dtype=jnp.int32)
        rank_of = units // slice_width
        holder = jnp.sum((inclusive[None, :] <= rank_of[:, None]).astype(jnp.int32), axis=1)
        source_col = (holder * SLOT + units - rank_of * slice_width).astype(jnp.int32)
        full = jnp.take(hid_rows, source_col, axis=1)
        partial_value = lax.dot_general(full, tok_rows, (((0,), (0,)), ((), ())), preferred_element_type=jnp.float32)
        return carry_sum + partial_value, grad_rows

    start = jnp.zeros((FF, D), jnp.float32)
    summed, grad_all = lax.scan(one_replica, start, jnp.arange(N_REP, dtype=jnp.int32))
    grad_hidden = grad_all.reshape(TOKENS, N_TP * SLOT)
    grad_weight = summed * (float(TOKENS) ** -0.5)
    return grad_hidden, grad_weight
```

```python
import functools

import jax
import jax.numpy as jnp
from jax import lax
from jax.experimental import pallas as pl
from jax.experimental.pallas import tpu as pltpu
from jax.sharding import PartitionSpec as P

FF = 7168
TOK, D, SLOT, COMMON = 1024, 2048, 512, 448
N_REP, N_TP = 32, 16
NEAR, FAR = 8, 4
ROWS = 224
GROUPS = ((0, 64), (64, 64), (128, 64), (192, 32))
PAD = 16
LOG_LEVELS = 14.999
FACTOR = float(N_REP * TOK) ** -0.5
F32, BF16, I16 = jnp.float32, jnp.bfloat16, jnp.int16
VMEM = pl.BlockSpec(memory_space=pltpu.VMEM)
SMEM = pl.BlockSpec(memory_space=pltpu.SMEM)


def layout(where, alive):
    replica = where[0]
    live = jnp.int32(0)
    for t in range(N_TP):
        live += alive[replica, t]
    width = lax.div(jnp.int32(FF), live)

    def holds(device):
        rank = jnp.int32(0)
        for t in range(N_TP):
            rank += jnp.where(t < device, alive[replica, t], 0)
        return alive[replica, device], rank * width

    return width, holds


def selection(width, held, first_wanted):
    is_alive, first_held = held
    rows = lax.broadcasted_iota(jnp.int32, (SLOT, COMMON), 0)
    cols = lax.broadcasted_iota(jnp.int32, (SLOT, COMMON), 1)
    shift = jnp.where(is_alive == 1, first_wanted - first_held, 4 * FF)
    return ((rows - cols == shift) & (rows < width)).astype(F32).astype(BF16)


def pick(own, other, sel_own, sel_other):
    got = jnp.dot(own, sel_own, preferred_element_type=F32)
    got += jnp.dot(other, sel_other, preferred_element_type=F32)
    return got.astype(BF16)


def windows_kernel(where, alive, own, other, right, left):
    width, holds = layout(where, alive)
    me = where[1]
    mine, theirs = holds(me), holds(me ^ 1)
    for out, to in ((right, me + 2), (left, me - 2)):
        first = to * COMMON
        sels = selection(width, mine, first), selection(width, theirs, first)
        for i in range(0, TOK, 256):
            out[i : i + 256] = pick(own[i : i + 256], other[i : i + 256], *sels)


def hidden_kernel(where, alive, grad, weight, own, other, grad_hidden, grad_t, local):
    width, holds = layout(where, alive)
    me = where[1]
    mine, theirs = holds(me), holds(me ^ 1)
    block = grad[...]
    product = lax.dot_general(block, weight[...], (((1,), (1,)), ((), ())), preferred_element_type=F32)
    cols = lax.broadcasted_iota(jnp.int32, product.shape, 1)
    limit = jnp.where(mine[0] == 1, width, 0)
    grad_hidden[...] = jnp.where(cols < limit, product, 0.0).astype(BF16)
    first = me * COMMON
    local[...] = pick(
        own[...], other[...], selection(width, mine, first), selection(width, theirs, first)
    )
    grad_t[...] = block.T


def steps_of(most):
    return jnp.ceil(256.0 * (jnp.log2(jnp.maximum(most, 1e-30)) - LOG_LEVELS))


def coded(value, inverse):
    return jnp.round(value * inverse).astype(jnp.int32).astype(I16)


def fold(product):
    groups = [product[:, c * 128 : c * 128 + 128] for c in range(3)]
    last = product[:, 384:]
    return groups + [last[:32] + pltpu.roll(last[32:], 64, 1)]


def tallest(value):
    return jnp.max(jnp.abs(value).reshape(value.shape[0] // 8, 8, 128), axis=0)


def write_code(out, index, blocks, folded, most):
    steps = [steps_of(jnp.max(m, axis=0, keepdims=True)) for m in most]
    inverse = [jnp.exp2(step * (-1.0 / 256.0)) for step in steps]
    for block in range(blocks):
        for (row, rows), inv in zip(GROUPS, inverse):
            r = block * ROWS + row
            out[index, r : r + rows] = coded(folded(r, rows), inv)
    head = jnp.concatenate(steps + [jnp.zeros((PAD - len(steps), 128), F32)], axis=0)
    out[index, blocks * ROWS :] = head.astype(jnp.int32).astype(I16)


def read_steps(got, index, blocks):
    head = got[index, blocks * ROWS :].astype(jnp.int32).astype(F32)
    return jnp.exp2(head * (1.0 / 256.0))


def read_sum(got, sources, steps, r, rows, group):
    value = None
    for k in range(sources):
        term = got[k, r : r + rows].astype(jnp.int32).astype(F32) * steps[k][group : group + 1]
        value = term if value is None else value + term
    return value


def partial_kernel(grad_t, local, from_left, from_right, out, common, folded):
    common[:, :COMMON] = local[...] + from_left[...] + from_right[...]
    common[:, COMMON:] = jnp.zeros((TOK, SLOT - COMMON), BF16)
    step = 256
    most = [[None] * len(GROUPS) for _ in range(NEAR)]
    for f in range(0, D, step):
        got = jnp.dot(grad_t[f : f + step], common[...], preferred_element_type=F32)
        for owner in range(f // 64, (f + step) // 64):
            far, near = owner // NEAR, owner % NEAR
            parts = fold(got[owner * 64 - f : owner * 64 - f + 64])
            for g, ((row, rows), part) in enumerate(zip(GROUPS, parts)):
                folded[near, far * ROWS + row : far * ROWS + row + rows] = part
                big = tallest(part)
                most[near][g] = big if far == 0 else jnp.maximum(most[near][g], big)
    for near in range(NEAR):
        write_code(out, near, FAR, lambda r, rows: folded[near, r : r + rows], most[near])


def middle_kernel(got, out, folded):
    steps = [read_steps(got, k, FAR) for k in range(NEAR)]
    for far in range(FAR):
        most = []
        for g, (row, rows) in enumerate(GROUPS):
            value = read_sum(got, NEAR, steps, far * ROWS + row, rows, g)
            folded[row : row + rows] = value
            most.append(tallest(value))
        write_code(out, far, 1, lambda r, rows: folded[r : r + rows], most)


def final_kernel(got, out):
    steps = [read_steps(got, k, 1) * FACTOR for k in range(FAR)]
    parts = [read_sum(got, FAR, steps, row, rows, g) for g, (row, rows) in enumerate(GROUPS)]
    for c in range(3):
        out[:, c * 128 : c * 128 + 128] = parts[c]
    out[:32, 384:] = parts[3][:, :64]
    out[32:, 384:] = pltpu.roll(parts[3], 64, 1)[:, :64]


def shape(dims, kind):
    return jax.ShapeDtypeStruct(dims, kind)


def params(mib):
    return pltpu.CompilerParams(vmem_limit_bytes=mib << 20)


def local(hidden, grad_out, weight, alive):
    where = jnp.stack([lax.axis_index("rep"), lax.axis_index("tp")]).astype(jnp.int32)
    other = lax.ppermute(hidden, "tp", [(t, t ^ 1) for t in range(N_TP)])
    right, left = pl.pallas_call(
        windows_kernel,
        out_shape=[shape((TOK, COMMON), BF16)] * 2,
        in_specs=[SMEM, SMEM, VMEM, VMEM],
        out_specs=[VMEM, VMEM],
        compiler_params=params(24),
        name="windows",
    )(where, alive, hidden, other)
    from_left = lax.ppermute(right, "tp", [(t, t + 2) for t in range(14) if t % 2 == 0 or t >= 6])
    from_right = lax.ppermute(left, "tp", [(t, t - 2) for t in range(2, 16) if t % 2 == 1 or t <= 8])
    step = 256
    grad_hidden, grad_t, own = pl.pallas_call(
        hidden_kernel,
        grid=(TOK // step,),
        out_shape=[shape((TOK, SLOT), BF16), shape((D, TOK), BF16), shape((TOK, COMMON), BF16)],
        in_specs=[
            SMEM,
            SMEM,
            pl.BlockSpec((step, D), lambda i: (i, 0)),
            pl.BlockSpec((SLOT, D), lambda i: (0, 0)),
            pl.BlockSpec((step, SLOT), lambda i: (i, 0)),
            pl.BlockSpec((step, SLOT), lambda i: (i, 0)),
        ],
        out_specs=[
            pl.BlockSpec((step, SLOT), lambda i: (i, 0)),
            pl.BlockSpec((D, step), lambda i: (0, i)),
            pl.BlockSpec((step, COMMON), lambda i: (i, 0)),
        ],
        compiler_params=params(24),
        cost_estimate=pl.CostEstimate(flops=2 * TOK * SLOT * (D + 2 * COMMON), bytes_accessed=16 << 20, transcendentals=0),
        name="hidden_grad",
    )(where, alive, grad_out, weight[0], hidden, other)
    payload = pl.pallas_call(
        partial_kernel,
        out_shape=shape((NEAR, FAR * ROWS + PAD, 128), I16),
        in_specs=[VMEM] * 4,
        out_specs=VMEM,
        scratch_shapes=[pltpu.VMEM((TOK, SLOT), BF16), pltpu.VMEM((NEAR, FAR * ROWS, 128), F32)],
        compiler_params=params(32),
        name="partial",
    )(grad_t, own, from_left, from_right)
    payload = lax.all_to_all(
        payload, "rep", 0, 0, axis_index_groups=[[f * NEAR + n for n in range(NEAR)] for f in range(FAR)]
    )
    payload = pl.pallas_call(
        middle_kernel,
        out_shape=shape((FAR, ROWS + PAD, 128), I16),
        in_specs=[VMEM],
        out_specs=VMEM,
        scratch_shapes=[pltpu.VMEM((ROWS, 128), F32)],
        compiler_params=params(16),
        name="middle",
    )(payload)
    payload = lax.all_to_all(
        payload, "rep", 0, 0, axis_index_groups=[[f * NEAR + n for f in range(FAR)] for n in range(NEAR)]
    )
    grad_weight_t = pl.pallas_call(
        final_kernel,
        out_shape=shape((64, COMMON), F32),
        in_specs=[VMEM],
        out_specs=VMEM,
        compiler_params=params(16),
        name="final",
    )(payload)
    return grad_hidden, grad_weight_t.T


def solution(mesh):
    return jax.shard_map(
        local,
        mesh=mesh,
        in_specs=(P("rep", "tp"), P("rep", None), P("rep", "tp", None), P()),
        out_specs=(P("rep", "tp"), P("tp", "rep")),
        check_vma=False,
    )
```

```python
import functools

import jax
import jax.numpy as jnp
from jax import lax
from jax.experimental import pallas as pl
from jax.experimental.pallas import tpu as pltpu
from jax.sharding import PartitionSpec as P

FF = 7168
TOK, D, SLOT, COMMON = 1024, 2048, 512, 448
N_REP, N_TP = 32, 16
NEAR, FAR = 8, 4
ROWS = 224
GROUPS = ((0, 64), (64, 64), (128, 64), (192, 32))
PAD = 16
LOG_LEVELS = 14.999
FACTOR = float(N_REP * TOK) ** -0.5
F32, BF16, I16 = jnp.float32, jnp.bfloat16, jnp.int16
VMEM = pl.BlockSpec(memory_space=pltpu.VMEM)
SMEM = pl.BlockSpec(memory_space=pltpu.SMEM)


def layout(where, alive):
    replica = where[0]
    live = jnp.int32(0)
    for t in range(N_TP):
        live += alive[t, replica]
    width = lax.div(jnp.int32(FF), live)

    def holds(device):
        rank = jnp.int32(0)
        for t in range(N_TP):
            rank += jnp.where(t < device, alive[t, replica], 0)
        return alive[device, replica], rank * width

    return width, holds


def selection(width, held, first_wanted):
    is_alive, first_held = held
    wanted = lax.broadcasted_iota(jnp.int32, (COMMON, SLOT), 0)
    cols = lax.broadcasted_iota(jnp.int32, (COMMON, SLOT), 1)
    shift = jnp.where(is_alive == 1, first_wanted - first_held, 4 * FF)
    return ((cols - wanted == shift) & (cols < width)).astype(F32).astype(BF16)


def across(a, b):
    return lax.dot_general(a, b, (((1,), (1,)), ((), ())), preferred_element_type=F32)


def even_odd(me, even, odd):
    return me + jnp.where(me % 2 == 0, even, odd)


def early_kernel(where, alive, own, out, select):
    @pl.when(pl.program_id(0) == 0)
    def _():
        width, holds = layout(where, alive)
        me = where[1]
        select[...] = selection(width, holds(me), even_odd(me, -2, 2) * COMMON)

    out[...] = across(select[...], own[...]).astype(BF16)


def late_kernel(where, alive, own, other, out, select):
    @pl.when(pl.program_id(0) == 0)
    def _():
        width, holds = layout(where, alive)
        me = where[1]
        first = even_odd(me, 2, -2) * COMMON
        select[0] = selection(width, holds(me), first)
        select[1] = selection(width, holds(me ^ 1), first)

    out[...] = (across(select[0], own[...]) + across(select[1], other[...])).astype(BF16)


def hidden_kernel(where, alive, grad, weight, own, other, grad_hidden, grad_t, local, select):
    width, holds = layout(where, alive)
    me = where[1]
    mine = holds(me)

    @pl.when(pl.program_id(0) == 0)
    def _():
        select[0] = selection(width, mine, me * COMMON)
        select[1] = selection(width, holds(me ^ 1), me * COMMON)

    block = grad[...]
    product = across(block, weight[...])
    cols = lax.broadcasted_iota(jnp.int32, product.shape, 1)
    limit = jnp.where(mine[0] == 1, width, 0)
    grad_hidden[...] = jnp.where(cols < limit, product, 0.0).astype(BF16)
    local[...] = (across(select[0], own[...]) + across(select[1], other[...])).astype(BF16)
    grad_t[...] = block.T


def steps_of(most):
    return jnp.ceil(256.0 * (jnp.log2(jnp.maximum(most, 1e-30)) - LOG_LEVELS))


def coded(value, inverse):
    return jnp.round(value * inverse).astype(jnp.int32).astype(I16)


def fold(product):
    groups = [product[:, c * 128 : c * 128 + 128] for c in range(3)]
    last = product[:, 384:]
    return groups + [last[:32] + pltpu.roll(last[32:], 64, 1)]


def tallest(value):
    return jnp.max(jnp.abs(value).reshape(value.shape[0] // 8, 8, 128), axis=0)


def write_code(out, index, blocks, folded, most):
    steps = [steps_of(jnp.max(m, axis=0, keepdims=True)) for m in most]
    inverse = [jnp.exp2(step * (-1.0 / 256.0)) for step in steps]
    for block in range(blocks):
        for (row, rows), inv in zip(GROUPS, inverse):
            r = block * ROWS + row
            out[index, r : r + rows] = coded(folded(r, rows), inv)
    head = jnp.concatenate(steps + [jnp.zeros((PAD - len(steps), 128), F32)], axis=0)
    out[index, blocks * ROWS :] = head.astype(jnp.int32).astype(I16)


def read_steps(got, index, blocks):
    head = got[index, blocks * ROWS :].astype(jnp.int32).astype(F32)
    return jnp.exp2(head * (1.0 / 256.0))


def read_sum(got, sources, steps, r, rows, group):
    value = None
    for k in range(sources):
        term = got[k, r : r + rows].astype(jnp.int32).astype(F32) * steps[k][group : group + 1]
        value = term if value is None else value + term
    return value


def partial_kernel(grad_t, local, early, late, out, common, folded, most):
    step = pl.program_id(0)

    @pl.when(step == 0)
    def _():
        common[:COMMON] = local[...] + early[...] + late[...]
        common[COMMON:] = jnp.zeros((SLOT - COMMON, TOK), BF16)
        most[...] = jnp.zeros(most.shape, F32)

    got = across(grad_t[...], common[...])
    for near in range(NEAR):
        for g, ((row, rows), part) in enumerate(zip(GROUPS, fold(got[near * 64 : near * 64 + 64]))):
            folded[step, near, row : row + rows] = part
            most[near, g] = jnp.maximum(most[near, g], tallest(part))

    @pl.when(step == FAR - 1)
    def _():
        for near in range(NEAR):
            write_code(
                out,
                near,
                FAR,
                lambda r, rows: folded[r // ROWS, near, r % ROWS : r % ROWS + rows],
                [most[near, g] for g in range(len(GROUPS))],
            )


def middle_kernel(got, out, folded):
    steps = [read_steps(got, k, FAR) for k in range(NEAR)]
    for far in range(FAR):
        most = []
        for g, (row, rows) in enumerate(GROUPS):
            value = read_sum(got, NEAR, steps, far * ROWS + row, rows, g)
            folded[row : row + rows] = value
            most.append(tallest(value))
        write_code(out, far, 1, lambda r, rows: folded[r : r + rows], most)


def final_kernel(got, out):
    steps = [read_steps(got, k, 1) * FACTOR for k in range(FAR)]
    parts = [read_sum(got, FAR, steps, row, rows, g) for g, (row, rows) in enumerate(GROUPS)]
    for c in range(3):
        out[:, c * 128 : c * 128 + 128] = parts[c]
    out[:32, 384:] = parts[3][:, :64]
    out[32:, 384:] = pltpu.roll(parts[3], 64, 1)[:, :64]


def shape(dims, kind):
    return jax.ShapeDtypeStruct(dims, kind)


def params(mib):
    return pltpu.CompilerParams(vmem_limit_bytes=mib << 20)


def block(dims, index):
    return pl.BlockSpec(dims, index)


def local(hidden, grad_out, weight, alive):
    where = jnp.stack([lax.axis_index("rep"), lax.axis_index("tp")]).astype(jnp.int32)
    alive = alive.T
    other = lax.ppermute(hidden, "tp", [(t, t ^ 1) for t in range(N_TP)])
    step = 256
    grid = (TOK // step,)
    tokens = block((step, SLOT), lambda i: (i, 0))
    window = block((COMMON, step), lambda i: (0, i))
    early = pl.pallas_call(
        early_kernel,
        grid=grid,
        out_shape=shape((COMMON, TOK), BF16),
        in_specs=[SMEM, SMEM, tokens],
        out_specs=window,
        scratch_shapes=[pltpu.VMEM((COMMON, SLOT), BF16)],
        compiler_params=params(56),
        name="early_window",
    )(where, alive, hidden)
    early = lax.ppermute(early, "tp", [(t, t + 2) for t in range(7, 14, 2)] + [(t, t - 2) for t in range(2, 9, 2)])
    late = pl.pallas_call(
        late_kernel,
        grid=grid,
        out_shape=shape((COMMON, TOK), BF16),
        in_specs=[SMEM, SMEM, tokens, tokens],
        out_specs=window,
        scratch_shapes=[pltpu.VMEM((2, COMMON, SLOT), BF16)],
        compiler_params=params(24),
        name="late_window",
    )(where, alive, hidden, other)
    late = lax.ppermute(late, "tp", [(t, t + 2) for t in range(0, 14, 2)] + [(t, t - 2) for t in range(3, 16, 2)])
    grad_hidden, grad_t, own = pl.pallas_call(
        hidden_kernel,
        grid=grid,
        out_shape=[shape((TOK, SLOT), BF16), shape((D, TOK), BF16), shape((COMMON, TOK), BF16)],
        in_specs=[SMEM, SMEM, block((step, D), lambda i: (i, 0)), block((SLOT, D), lambda i: (0, 0)), tokens, tokens],
        out_specs=[tokens, block((D, step), lambda i: (0, i)), window],
        scratch_shapes=[pltpu.VMEM((2, COMMON, SLOT), BF16)],
        compiler_params=params(28),
        cost_estimate=pl.CostEstimate(flops=2 * TOK * SLOT * (D + 2 * COMMON), bytes_accessed=16 << 20, transcendentals=0),
        name="hidden_grad",
    )(where, alive, grad_out, weight[0], hidden, other)
    whole = block((COMMON, TOK), lambda i: (0, 0))
    payload = pl.pallas_call(
        partial_kernel,
        grid=(FAR,),
        out_shape=shape((NEAR, FAR * ROWS + PAD, 128), I16),
        in_specs=[block((D // FAR, TOK), lambda i: (i, 0)), whole, whole, whole],
        out_specs=block((NEAR, FAR * ROWS + PAD, 128), lambda i: (0, 0, 0)),
        scratch_shapes=[
            pltpu.VMEM((SLOT, TOK), BF16),
            pltpu.VMEM((FAR, NEAR, ROWS, 128), F32),
            pltpu.VMEM((NEAR, len(GROUPS), 8, 128), F32),
        ],
        compiler_params=params(32),
        name="partial",
    )(grad_t, own, early, late)
    payload = lax.all_to_all(
        payload, "rep", 0, 0, axis_index_groups=[[f * NEAR + n for n in range(NEAR)] for f in range(FAR)]
    )
    payload = pl.pallas_call(
        middle_kernel,
        out_shape=shape((FAR, ROWS + PAD, 128), I16),
        in_specs=[VMEM],
        out_specs=VMEM,
        scratch_shapes=[pltpu.VMEM((ROWS, 128), F32)],
        compiler_params=params(16),
        name="middle",
    )(payload)
    payload = lax.all_to_all(
        payload, "rep", 0, 0, axis_index_groups=[[f * NEAR + n for f in range(FAR)] for n in range(NEAR)]
    )
    grad_weight_t = pl.pallas_call(
        final_kernel,
        out_shape=shape((64, COMMON), F32),
        in_specs=[VMEM],
        out_specs=VMEM,
        compiler_params=params(16),
        name="final",
    )(payload)
    return grad_hidden, grad_weight_t.T


def solution(mesh):
    return jax.shard_map(
        local,
        mesh=mesh,
        in_specs=(P("rep", "tp"), P("rep", None), P("rep", "tp", None), P()),
        out_specs=(P("rep", "tp"), P("tp", "rep")),
        check_vma=False,
    )
```

```python
import functools

import jax
import jax.numpy as jnp
from jax import lax
from jax.experimental import pallas as pl
from jax.experimental.pallas import tpu as pltpu
from jax.sharding import PartitionSpec as P

FF = 7168
TOK, D, SLOT, COMMON = 1024, 2048, 512, 448
N_REP, N_TP = 32, 16
NEAR, FAR = 8, 4
ROWS = 224
GROUPS = ((0, 64), (64, 64), (128, 64), (192, 32))
PAD = 16
LOG_LEVELS = 14.999
FACTOR = float(N_REP * TOK) ** -0.5
F32, BF16, I16 = jnp.float32, jnp.bfloat16, jnp.int16
VMEM = pl.BlockSpec(memory_space=pltpu.VMEM)
SMEM = pl.BlockSpec(memory_space=pltpu.SMEM)


def layout(where, alive):
    replica = where[0]
    live = jnp.int32(0)
    for t in range(N_TP):
        live += alive[t, replica]
    width = lax.div(jnp.int32(FF), live)

    def holds(device):
        rank = jnp.int32(0)
        for t in range(N_TP):
            rank += jnp.where(t < device, alive[t, replica], 0)
        return alive[device, replica], rank * width

    return width, holds


def selection(width, held, first_wanted):
    is_alive, first_held = held
    wanted = lax.broadcasted_iota(jnp.int32, (COMMON, SLOT), 0)
    cols = lax.broadcasted_iota(jnp.int32, (COMMON, SLOT), 1)
    shift = jnp.where(is_alive == 1, first_wanted - first_held, 4 * FF)
    return ((cols - wanted == shift) & (cols < width)).astype(F32).astype(BF16)


def across(a, b):
    return lax.dot_general(a, b, (((1,), (1,)), ((), ())), preferred_element_type=F32)


def even_odd(me, even, odd):
    return me + jnp.where(me % 2 == 0, even, odd)


def merge_kernel(where, alive, local, early, out):
    width, holds = layout(where, alive)
    me = where[1]
    source = jnp.clip(even_odd(me, 2, -2), 0, N_TP - 1)
    out[...] = local[...] + across(selection(width, holds(source), me * COMMON), early[...]).astype(BF16)


def late_kernel(where, alive, own, other, out, select):
    @pl.when(pl.program_id(0) == 0)
    def _():
        width, holds = layout(where, alive)
        me = where[1]
        first = even_odd(me, 2, -2) * COMMON
        select[0] = selection(width, holds(me), first)
        select[1] = selection(width, holds(me ^ 1), first)

    out[...] = (across(select[0], own[...]) + across(select[1], other[...])).astype(BF16)


def hidden_kernel(where, alive, grad, weight, own, other, grad_hidden, grad_t, local, select):
    width, holds = layout(where, alive)
    me = where[1]
    mine = holds(me)

    @pl.when(pl.program_id(0) == 0)
    def _():
        select[0] = selection(width, mine, me * COMMON)
        select[1] = selection(width, holds(me ^ 1), me * COMMON)

    block = grad[...]
    product = across(block, weight[...])
    cols = lax.broadcasted_iota(jnp.int32, product.shape, 1)
    limit = jnp.where(mine[0] == 1, width, 0)
    grad_hidden[...] = jnp.where(cols < limit, product, 0.0).astype(BF16)
    local[...] = (across(select[0], own[...]) + across(select[1], other[...])).astype(BF16)
    grad_t[...] = block.T


def steps_of(most):
    return jnp.ceil(256.0 * (jnp.log2(jnp.maximum(most, 1e-30)) - LOG_LEVELS))


def coded(value, inverse):
    return jnp.round(value * inverse).astype(jnp.int32).astype(I16)


def fold(product):
    groups = [product[:, c * 128 : c * 128 + 128] for c in range(3)]
    last = product[:, 384:]
    return groups + [last[:32] + pltpu.roll(last[32:], 64, 1)]


def tallest(value):
    return jnp.max(jnp.abs(value).reshape(value.shape[0] // 8, 8, 128), axis=0)


def write_code(out, index, blocks, folded, most):
    steps = [steps_of(jnp.max(m, axis=0, keepdims=True)) for m in most]
    inverse = [jnp.exp2(step * (-1.0 / 256.0)) for step in steps]
    for block in range(blocks):
        for (row, rows), inv in zip(GROUPS, inverse):
            r = block * ROWS + row
            out[index, r : r + rows] = coded(folded(r, rows), inv)
    head = jnp.concatenate(steps + [jnp.zeros((PAD - len(steps), 128), F32)], axis=0)
    out[index, blocks * ROWS :] = head.astype(jnp.int32).astype(I16)


def read_steps(got, index, blocks):
    head = got[index, blocks * ROWS :].astype(jnp.int32).astype(F32)
    return jnp.exp2(head * (1.0 / 256.0))


def read_sum(got, sources, steps, r, rows, group):
    value = None
    for k in range(sources):
        term = got[k, r : r + rows].astype(jnp.int32).astype(F32) * steps[k][group : group + 1]
        value = term if value is None else value + term
    return value


def partial_kernel(grad_t, local, late, out, common, folded):
    common[:COMMON] = local[...] + late[...]
    common[COMMON:] = jnp.zeros((SLOT - COMMON, TOK), BF16)
    most = [[None] * len(GROUPS) for _ in range(NEAR)]
    step = 256
    for f in range(0, D, step):
        got = across(grad_t[f : f + step], common[...])
        for owner in range(f // 64, (f + step) // 64):
            far, near = owner // NEAR, owner % NEAR
            parts = fold(got[owner * 64 - f : owner * 64 - f + 64])
            for g, ((row, rows), part) in enumerate(zip(GROUPS, parts)):
                folded[near, far * ROWS + row : far * ROWS + row + rows] = part
                big = tallest(part)
                most[near][g] = big if far == 0 else jnp.maximum(most[near][g], big)
    for near in range(NEAR):
        write_code(out, near, FAR, lambda r, rows: folded[near, r : r + rows], most[near])


def middle_kernel(got, out, folded):
    steps = [read_steps(got, k, FAR) for k in range(NEAR)]
    for far in range(FAR):
        most = []
        for g, (row, rows) in enumerate(GROUPS):
            value = read_sum(got, NEAR, steps, far * ROWS + row, rows, g)
            folded[row : row + rows] = value
            most.append(tallest(value))
        write_code(out, far, 1, lambda r, rows: folded[r : r + rows], most)


def final_kernel(got, out):
    steps = [read_steps(got, k, 1) * FACTOR for k in range(FAR)]
    parts = [read_sum(got, FAR, steps, row, rows, g) for g, (row, rows) in enumerate(GROUPS)]
    for c in range(3):
        out[:, c * 128 : c * 128 + 128] = parts[c]
    out[:32, 384:] = parts[3][:, :64]
    out[32:, 384:] = pltpu.roll(parts[3], 64, 1)[:, :64]


def shape(dims, kind):
    return jax.ShapeDtypeStruct(dims, kind)


def params(mib):
    return pltpu.CompilerParams(vmem_limit_bytes=mib << 20)


def block(dims, index):
    return pl.BlockSpec(dims, index)


def local(hidden, grad_out, weight, alive):
    where = jnp.stack([lax.axis_index("rep"), lax.axis_index("tp")]).astype(jnp.int32)
    alive = alive.T
    other = lax.ppermute(hidden, "tp", [(t, t ^ 1) for t in range(N_TP)])
    step = 256
    grid = (TOK // step,)
    tokens = block((step, SLOT), lambda i: (i, 0))
    window = block((COMMON, step), lambda i: (0, i))
    early = lax.ppermute(hidden, "tp", [(t, t + 2) for t in range(7, 14, 2)] + [(t, t - 2) for t in range(2, 9, 2)])
    late = pl.pallas_call(
        late_kernel,
        grid=grid,
        out_shape=shape((COMMON, TOK), BF16),
        in_specs=[SMEM, SMEM, tokens, tokens],
        out_specs=window,
        scratch_shapes=[pltpu.VMEM((2, COMMON, SLOT), BF16)],
        compiler_params=params(24),
        name="late_window",
    )(where, alive, hidden, other)
    late = lax.ppermute(late, "tp", [(t, t + 2) for t in range(0, 14, 2)] + [(t, t - 2) for t in range(3, 16, 2)])
    grad_hidden, grad_t, own = pl.pallas_call(
        hidden_kernel,
        grid=grid,
        out_shape=[shape((TOK, SLOT), BF16), shape((D, TOK), BF16), shape((COMMON, TOK), BF16)],
        in_specs=[SMEM, SMEM, block((step, D), lambda i: (i, 0)), block((SLOT, D), lambda i: (0, 0)), tokens, tokens],
        out_specs=[tokens, block((D, step), lambda i: (0, i)), window],
        scratch_shapes=[pltpu.VMEM((2, COMMON, SLOT), BF16)],
        compiler_params=params(28),
        cost_estimate=pl.CostEstimate(flops=2 * TOK * SLOT * (D + 2 * COMMON), bytes_accessed=16 << 20, transcendentals=0),
        name="hidden_grad",
    )(where, alive, grad_out, weight[0], hidden, other)
    own = pl.pallas_call(
        merge_kernel,
        out_shape=shape((COMMON, TOK), BF16),
        in_specs=[SMEM, SMEM, VMEM, VMEM],
        out_specs=VMEM,
        compiler_params=params(24),
        name="merge",
    )(where, alive, own, early)
    payload = pl.pallas_call(
        partial_kernel,
        out_shape=shape((NEAR, FAR * ROWS + PAD, 128), I16),
        in_specs=[VMEM] * 3,
        out_specs=VMEM,
        scratch_shapes=[pltpu.VMEM((SLOT, TOK), BF16), pltpu.VMEM((NEAR, FAR * ROWS, 128), F32)],
        compiler_params=params(32),
        name="partial",
    )(grad_t, own, late)
    payload = lax.all_to_all(
        payload, "rep", 0, 0, axis_index_groups=[[f * NEAR + n for n in range(NEAR)] for f in range(FAR)]
    )
    payload = pl.pallas_call(
        middle_kernel,
        out_shape=shape((FAR, ROWS + PAD, 128), I16),
        in_specs=[VMEM],
        out_specs=VMEM,
        scratch_shapes=[pltpu.VMEM((ROWS, 128), F32)],
        compiler_params=params(16),
        name="middle",
    )(payload)
    payload = lax.all_to_all(
        payload, "rep", 0, 0, axis_index_groups=[[f * NEAR + n for f in range(FAR)] for n in range(NEAR)]
    )
    grad_weight_t = pl.pallas_call(
        final_kernel,
        out_shape=shape((64, COMMON), F32),
        in_specs=[VMEM],
        out_specs=VMEM,
        compiler_params=params(16),
        name="final",
    )(payload)
    return grad_hidden, grad_weight_t.T


def solution(mesh):
    return jax.shard_map(
        local,
        mesh=mesh,
        in_specs=(P("rep", "tp"), P("rep", None), P("rep", "tp", None), P()),
        out_specs=(P("rep", "tp"), P("tp", "rep")),
        check_vma=False,
    )
```

```python
import functools

import jax
import jax.numpy as jnp
from jax import lax
from jax.experimental import pallas as pl
from jax.experimental.pallas import tpu as pltpu
from jax.sharding import PartitionSpec as P

FF = 7168
TOK, D, SLOT, COMMON = 1024, 2048, 512, 448
N_REP, N_TP = 32, 16
NEAR, FAR = 8, 4
ROWS = 224
GROUPS = ((0, 64), (64, 64), (128, 64), (192, 32))
PAD = 16
LOG_LEVELS = 14.999
MID = 64
WIDTH, LIMIT, LATE_OWN, LATE_OTHER, LOCAL_OWN, LOCAL_OTHER, EARLY, MIDDLE, ODD = range(9)
FACTOR = float(N_REP * TOK) ** -0.5
F32, BF16, I16 = jnp.float32, jnp.bfloat16, jnp.int16
VMEM = pl.BlockSpec(memory_space=pltpu.VMEM)
SMEM = pl.BlockSpec(memory_space=pltpu.SMEM)


def plan_kernel(alive, plan):
    replica, me = lax.axis_index("rep"), lax.axis_index("tp")
    live = jnp.int32(0)
    for t in range(N_TP):
        live += alive[t, replica]
    width = lax.div(jnp.int32(FF), live)

    def shift(device, slot):
        rank = jnp.int32(0)
        for t in range(N_TP):
            rank += jnp.where(t < device, alive[t, replica], 0)
        return jnp.where(alive[device, replica] == 1, slot * COMMON - rank * width, 4 * FF)

    other = me ^ 1
    back = even_odd(me, -2, 2)
    away = even_odd(me, 2, -2)
    plan[WIDTH] = width
    plan[LIMIT] = jnp.where(alive[me, replica] == 1, width, 0)
    plan[LATE_OWN] = shift(me, away)
    plan[LATE_OTHER] = shift(other, away)
    plan[LOCAL_OWN] = shift(me, me)
    plan[LOCAL_OTHER] = shift(other, me)
    plan[EARLY] = shift(jnp.clip(away, 0, N_TP - 1), me)
    plan[MIDDLE] = shift(me, back) + jnp.where(me % 2 == 0, COMMON - MID, 0)
    plan[ODD] = me % 2


def selection(width, shift, wanted=COMMON):
    ahead = lax.broadcasted_iota(jnp.int32, (wanted, SLOT), 1) - lax.broadcasted_iota(jnp.int32, (wanted, SLOT), 0)
    cols = lax.broadcasted_iota(jnp.int32, (wanted, SLOT), 1)
    return ((ahead == shift) & (cols < width)).astype(F32).astype(BF16)


def across(a, b):
    return lax.dot_general(a, b, (((1,), (1,)), ((), ())), preferred_element_type=F32)


def even_odd(me, even, odd):
    return me + jnp.where(me % 2 == 0, even, odd)


def late_kernel(plan, hidden, other, out, middle, own, sem):
    copy = pltpu.make_async_copy(hidden, own, sem)
    copy.start()
    width = plan[WIDTH]
    from_other = selection(width, plan[LATE_OTHER])
    from_own = selection(width, plan[LATE_OWN])
    from_middle = selection(width, plan[MIDDLE], MID)
    copy.wait()
    for i in range(0, TOK, 256):
        got = across(from_own, own[i : i + 256]) + across(from_other, other[i : i + 256])
        out[:, i : i + 256] = got.astype(BF16)
        middle[:, i : i + 256] = across(from_middle, own[i : i + 256]).astype(BF16)


def merge_kernel(plan, local, early, middle, out):
    out[...] = local[...] + across(selection(plan[WIDTH], plan[EARLY]), early[...]).astype(BF16)

    @pl.when(plan[ODD] == 1)
    def _():
        out[:MID] = out[:MID] + middle[...]

    @pl.when(plan[ODD] == 0)
    def _():
        out[COMMON - MID :] = out[COMMON - MID :] + middle[...]


def hidden_kernel(plan, grad, weight, own, other, grad_hidden, grad_t, local, select):
    @pl.when(pl.program_id(0) == 0)
    def _():
        select[0] = selection(plan[WIDTH], plan[LOCAL_OWN])
        select[1] = selection(plan[WIDTH], plan[LOCAL_OTHER])

    block = grad[...]
    product = across(block, weight[...])
    cols = lax.broadcasted_iota(jnp.int32, product.shape, 1)
    grad_hidden[...] = jnp.where(cols < plan[LIMIT], product, 0.0).astype(BF16)
    local[...] = (across(select[0], own[...]) + across(select[1], other[...])).astype(BF16)
    turned = block.T
    for owner in range(N_REP):
        row = (owner % NEAR * FAR + owner // NEAR) * 64
        grad_t[row : row + 64] = turned[owner * 64 : owner * 64 + 64]


def steps_of(most):
    return jnp.ceil(256.0 * (jnp.log2(jnp.maximum(most, 1e-30)) - LOG_LEVELS))


def coded(value, inverse):
    return jnp.round(value * inverse).astype(jnp.int32).astype(I16)


def fold(product):
    groups = [product[:, c * 128 : c * 128 + 128] for c in range(3)]
    last = product[:, 384:]
    return groups + [last[:32] + pltpu.roll(last[32:], 64, 1)]


def tallest(value):
    return jnp.max(jnp.abs(value).reshape(value.shape[0] // 8, 8, 128), axis=0)


def write_code(out, index, blocks, folded, most):
    steps = [steps_of(jnp.max(m, axis=0, keepdims=True)) for m in most]
    inverse = [jnp.exp2(step * (-1.0 / 256.0)) for step in steps]
    for block in range(blocks):
        for (row, rows), inv in zip(GROUPS, inverse):
            r = block * ROWS + row
            out[index, r : r + rows] = coded(folded(r, rows), inv)
    head = jnp.concatenate(steps + [jnp.zeros((PAD - len(steps), 128), F32)], axis=0)
    out[index, blocks * ROWS :] = head.astype(jnp.int32).astype(I16)


def read_steps(got, index, blocks):
    head = got[index, blocks * ROWS :].astype(jnp.int32).astype(F32)
    return jnp.exp2(head * (1.0 / 256.0))


def read_sum(got, sources, steps, r, rows, group):
    value = None
    for k in range(sources):
        term = got[k, r : r + rows].astype(jnp.int32).astype(F32) * steps[k][group : group + 1]
        value = term if value is None else value + term
    return value


def partial_kernel(grad_t, local, late, out, common, folded):
    common[:COMMON] = local[...] + late[...]
    common[COMMON:] = jnp.zeros((SLOT - COMMON, TOK), BF16)
    step = FAR * 64
    for near in range(NEAR):
        got = across(grad_t[near * step : near * step + step], common[...])
        most = [None] * len(GROUPS)
        for far in range(FAR):
            for g, ((row, rows), part) in enumerate(zip(GROUPS, fold(got[far * 64 : far * 64 + 64]))):
                folded[near, far * ROWS + row : far * ROWS + row + rows] = part
                big = tallest(part)
                most[g] = big if far == 0 else jnp.maximum(most[g], big)
        write_code(out, near, FAR, lambda r, rows: folded[near, r : r + rows], most)


def middle_kernel(got, out, folded):
    steps = [read_steps(got, k, FAR) for k in range(NEAR)]
    for far in range(FAR):
        most = []
        for g, (row, rows) in enumerate(GROUPS):
            value = read_sum(got, NEAR, steps, far * ROWS + row, rows, g)
            folded[row : row + rows] = value
            most.append(tallest(value))
        write_code(out, far, 1, lambda r, rows: folded[r : r + rows], most)


def final_kernel(got, out):
    steps = [read_steps(got, k, 1) * FACTOR for k in range(FAR)]
    parts = [read_sum(got, FAR, steps, row, rows, g) for g, (row, rows) in enumerate(GROUPS)]
    for c in range(3):
        out[:, c * 128 : c * 128 + 128] = parts[c]
    out[:32, 384:] = parts[3][:, :64]
    out[32:, 384:] = pltpu.roll(parts[3], 64, 1)[:, :64]


def shape(dims, kind):
    return jax.ShapeDtypeStruct(dims, kind)


def params(mib):
    return pltpu.CompilerParams(vmem_limit_bytes=mib << 20)


def block(dims, index):
    return pl.BlockSpec(dims, index)


def local(hidden, grad_out, weight, alive):
    other = lax.ppermute(hidden, "tp", [(t, t ^ 1) for t in range(N_TP)])
    early = lax.ppermute(hidden, "tp", [(t, t + 2) for t in (9, 11, 13)] + [(t, t - 2) for t in (2, 4, 6)])
    plan = pl.pallas_call(
        plan_kernel,
        out_shape=shape((16,), jnp.int32),
        in_specs=[SMEM],
        out_specs=SMEM,
        name="plan",
    )(alive.T)
    late, middle = pl.pallas_call(
        late_kernel,
        out_shape=[shape((COMMON, TOK), BF16), shape((MID, TOK), BF16)],
        in_specs=[SMEM, pl.BlockSpec(memory_space=pltpu.HBM), VMEM],
        out_specs=[VMEM, VMEM],
        scratch_shapes=[pltpu.VMEM((TOK, SLOT), BF16), pltpu.SemaphoreType.DMA],
        compiler_params=params(24),
        name="late_window",
    )(plan, hidden, other)
    late = lax.ppermute(late, "tp", [(t, t + 2) for t in range(0, 14, 2)] + [(t, t - 2) for t in range(3, 16, 2)])
    middle = lax.ppermute(middle, "tp", [(7, 9), (8, 6)])
    step = 256
    tokens = block((step, SLOT), lambda i: (i, 0))
    grad_hidden, grad_t, own = pl.pallas_call(
        hidden_kernel,
        grid=(TOK // step,),
        out_shape=[shape((TOK, SLOT), BF16), shape((D, TOK), BF16), shape((COMMON, TOK), BF16)],
        in_specs=[SMEM, block((step, D), lambda i: (i, 0)), block((SLOT, D), lambda i: (0, 0)), tokens, tokens],
        out_specs=[tokens, block((D, step), lambda i: (0, i)), block((COMMON, step), lambda i: (0, i))],
        scratch_shapes=[pltpu.VMEM((2, COMMON, SLOT), BF16)],
        compiler_params=params(28),
        cost_estimate=pl.CostEstimate(flops=2 * TOK * SLOT * (D + 2 * COMMON), bytes_accessed=16 << 20, transcendentals=0),
        name="hidden_grad",
    )(plan, grad_out, weight[0], hidden, other)
    own = pl.pallas_call(
        merge_kernel,
        out_shape=shape((COMMON, TOK), BF16),
        in_specs=[SMEM, VMEM, VMEM, VMEM],
        out_specs=VMEM,
        compiler_params=params(24),
        name="merge",
    )(plan, own, early, middle)
    payload = pl.pallas_call(
        partial_kernel,
        out_shape=shape((NEAR, FAR * ROWS + PAD, 128), I16),
        in_specs=[VMEM] * 3,
        out_specs=VMEM,
        scratch_shapes=[pltpu.VMEM((SLOT, TOK), BF16), pltpu.VMEM((NEAR, FAR * ROWS, 128), F32)],
        compiler_params=params(32),
        name="partial",
    )(grad_t, own, late)
    payload = lax.all_to_all(
        payload, "rep", 0, 0, axis_index_groups=[[f * NEAR + n for n in range(NEAR)] for f in range(FAR)]
    )
    payload = pl.pallas_call(
        middle_kernel,
        out_shape=shape((FAR, ROWS + PAD, 128), I16),
        in_specs=[VMEM],
        out_specs=VMEM,
        scratch_shapes=[pltpu.VMEM((ROWS, 128), F32)],
        compiler_params=params(16),
        name="middle",
    )(payload)
    payload = lax.all_to_all(
        payload, "rep", 0, 0, axis_index_groups=[[f * NEAR + n for f in range(FAR)] for n in range(NEAR)]
    )
    grad_weight_t = pl.pallas_call(
        final_kernel,
        out_shape=shape((64, COMMON), F32),
        in_specs=[VMEM],
        out_specs=VMEM,
        compiler_params=params(16),
        name="final",
    )(payload)
    return grad_hidden, grad_weight_t.T


def solution(mesh):
    return jax.shard_map(
        local,
        mesh=mesh,
        in_specs=(P("rep", "tp"), P("rep", None), P("rep", "tp", None), P()),
        out_specs=(P("rep", "tp"), P("tp", "rep")),
        check_vma=False,
    )
```

```python
import functools

import jax
import jax.numpy as jnp
from jax import lax
from jax.experimental import pallas as pl
from jax.experimental.pallas import tpu as pltpu
from jax.sharding import PartitionSpec as P

FF = 7168
TOK, D, SLOT, COMMON = 1024, 2048, 512, 448
N_REP, N_TP = 32, 16
NEAR, FAR = 8, 4
ROWS = 224
GROUPS = ((0, 64), (64, 64), (128, 64), (192, 32))
UNITS = ((0, 0, 128), (128, 256, 96), (224, 128, 128), (352, 352, 96))
PAD = 16
LOG_LEVELS = 14.999
MID = 64
WIDTH, LIMIT, LATE_OWN, LATE_OTHER, LOCAL_OWN, LOCAL_OTHER, EARLY, LIGHT, MIDDLE, ODD = range(10)
FACTOR = float(N_REP * TOK) ** -0.5
F32, BF16, I16 = jnp.float32, jnp.bfloat16, jnp.int16
VMEM = pl.BlockSpec(memory_space=pltpu.VMEM)
SMEM = pl.BlockSpec(memory_space=pltpu.SMEM)


def own_kernel(alive, own, plan, out, middle):
    replica, me = lax.axis_index("rep"), lax.axis_index("tp")
    live = jnp.int32(0)
    for t in range(N_TP):
        live += alive[t, replica]
    width = lax.div(jnp.int32(FF), live)

    def shift(device, slot):
        rank = jnp.int32(0)
        for t in range(N_TP):
            rank += jnp.where(t < device, alive[t, replica], 0)
        return jnp.where(alive[device, replica] == 1, slot * COMMON - rank * width, 4 * FF)

    other = me ^ 1
    back = even_odd(me, -2, 2)
    away = even_odd(me, 2, -2)
    plan[WIDTH] = width
    plan[LIMIT] = jnp.where(alive[me, replica] == 1, width, 0)
    plan[LATE_OWN] = shift(me, away)
    plan[LATE_OTHER] = shift(other, away)
    plan[LOCAL_OWN] = shift(me, me)
    plan[LOCAL_OTHER] = shift(other, me)
    plan[EARLY] = shift(jnp.clip(away, 0, N_TP - 1), me)
    plan[LIGHT] = shift(jnp.clip(even_odd(me, -1, 1), 0, N_TP - 1), me)
    plan[MIDDLE] = shift(me, back) + jnp.where(me % 2 == 0, COMMON - MID, 0)
    plan[ODD] = me % 2
    late = selection(width, plan[LATE_OWN])
    small = selection(width, plan[MIDDLE], MID)
    for i in range(0, TOK, 256):
        out[:, i : i + 256] = across(late, own[i : i + 256]).astype(BF16)
        middle[:, i : i + 256] = across(small, own[i : i + 256]).astype(BF16)


def selection(width, shift, wanted=COMMON):
    ahead = lax.broadcasted_iota(jnp.int32, (wanted, SLOT), 1) - lax.broadcasted_iota(jnp.int32, (wanted, SLOT), 0)
    cols = lax.broadcasted_iota(jnp.int32, (wanted, SLOT), 1)
    return ((ahead == shift) & (cols < width)).astype(F32).astype(BF16)


def across(a, b):
    return lax.dot_general(a, b, (((1,), (1,)), ((), ())), preferred_element_type=F32)


def even_odd(me, even, odd):
    return me + jnp.where(me % 2 == 0, even, odd)


def late_kernel(plan, own, other, out):
    late = selection(plan[WIDTH], plan[LATE_OTHER])
    for i in range(0, TOK, 256):
        out[:, i : i + 256] = own[:, i : i + 256] + across(late, other[i : i + 256]).astype(BF16)


def merge_kernel(plan, middle, light, early, local, out):
    width = plan[WIDTH]
    got = across(selection(width, plan[EARLY]), early[...])
    got += across(selection(width, plan[LIGHT]), light[...])
    out[...] = local[...] + got.astype(BF16)

    @pl.when(plan[ODD] == 1)
    def _():
        out[:MID] = out[:MID] + middle[...]

    @pl.when(plan[ODD] == 0)
    def _():
        out[COMMON - MID :] = out[COMMON - MID :] + middle[...]


def hidden_kernel(plan, grad, weight, own, other, grad_hidden, local, select):
    @pl.when(pl.program_id(0) == 0)
    def _():
        select[0] = selection(plan[WIDTH], plan[LOCAL_OWN])
        select[1] = selection(plan[WIDTH], plan[LOCAL_OTHER])

    block = grad[...]
    product = across(block, weight[...])
    cols = lax.broadcasted_iota(jnp.int32, product.shape, 1)
    grad_hidden[...] = jnp.where(cols < plan[LIMIT], product, 0.0).astype(BF16)
    local[...] = (across(select[0], own[...]) + across(select[1], other[...])).astype(BF16)


def steps_of(most):
    return jnp.ceil(256.0 * (jnp.log2(jnp.maximum(most, 1e-30)) - LOG_LEVELS))


def coded(value, inverse):
    return jnp.round(value * inverse).astype(jnp.int32).astype(I16)


def low_lanes(rows, below):
    return lax.broadcasted_iota(jnp.int32, (rows, 128), 1) < below


def fold(top, bottom):
    low = low_lanes(ROWS, 64)
    return jnp.where(low, top, pltpu.roll(bottom, 64, 1)), jnp.where(low, pltpu.roll(top, 64, 1), bottom)


def tallest(value):
    return jnp.max(jnp.abs(value).reshape(value.shape[0] // 8, 8, 128), axis=0)


def write_code(out, index, blocks, folded, most):
    steps = [steps_of(jnp.max(m, axis=0, keepdims=True)) for m in most]
    inverse = [jnp.exp2(step * (-1.0 / 256.0)) for step in steps]
    for block in range(blocks):
        for (row, rows), inv in zip(GROUPS, inverse):
            r = block * ROWS + row
            out[index, r : r + rows] = coded(folded(r, rows), inv)
    head = jnp.concatenate(steps + [jnp.zeros((PAD - len(steps), 128), F32)], axis=0)
    out[index, blocks * ROWS :] = head.astype(jnp.int32).astype(I16)


def read_steps(got, index, blocks):
    head = got[index, blocks * ROWS :].astype(jnp.int32).astype(F32)
    return jnp.exp2(head * (1.0 / 256.0))


def read_sum(got, sources, steps, r, rows, group):
    value = None
    for k in range(sources):
        term = got[k, r : r + rows].astype(jnp.int32).astype(F32) * steps[k][group : group + 1]
        value = term if value is None else value + term
    return value


def partial_kernel(grad, local, late, out, common, folded):
    for to, first, count in UNITS:
        common[to : to + count] = local[first : first + count] + late[first : first + count]
    wide = NEAR // 2 * 64
    for half in range(2):
        most = [[None] * len(GROUPS) for _ in range(NEAR)]
        for far in range(FAR):
            f = (far * 2 + half) * wide
            got = jnp.dot(common[...], grad[:, f : f + wide], preferred_element_type=F32)
            for c in range(0, wide, 128):
                near = half * (NEAR // 2) + c // 64
                for n, part in enumerate(fold(got[:ROWS, c : c + 128], got[ROWS:, c : c + 128]), near):
                    folded[n, far * ROWS : far * ROWS + ROWS] = part
                    for g, (row, rows) in enumerate(GROUPS):
                        big = tallest(part[row : row + rows])
                        most[n][g] = big if far == 0 else jnp.maximum(most[n][g], big)
        for n in range(half * (NEAR // 2), (half + 1) * (NEAR // 2)):
            write_code(out, n, FAR, lambda r, rows: folded[n, r : r + rows], most[n])


def middle_kernel(got, out, folded):
    steps = [read_steps(got, k, FAR) for k in range(NEAR)]
    for far in range(FAR):
        most = []
        for g, (row, rows) in enumerate(GROUPS):
            value = read_sum(got, NEAR, steps, far * ROWS + row, rows, g)
            folded[row : row + rows] = value
            most.append(tallest(value))
        write_code(out, far, 1, lambda r, rows: folded[r : r + rows], most)


def final_kernel(got, out, total):
    steps = [read_steps(got, k, 1) * FACTOR for k in range(FAR)]
    for g, (row, rows) in enumerate(GROUPS):
        total[row : row + rows] = read_sum(got, FAR, steps, row, rows, g)
    total[ROWS:] = jnp.zeros((256 - ROWS, 128), F32)
    turned = total[...].T
    out[:, :128] = turned[:64, :128]
    out[:, 128:256] = turned[64:, :128]
    rest = pltpu.roll(turned[64:, 128:], 96, 1)
    out[:, 256:384] = jnp.where(low_lanes(64, 96), turned[:64, 128:], rest)
    out[:, 384:] = rest[:, :64]


def shape(dims, kind):
    return jax.ShapeDtypeStruct(dims, kind)


def params(mib):
    return pltpu.CompilerParams(vmem_limit_bytes=mib << 20)


def block(dims, index):
    return pl.BlockSpec(dims, index)


def local(hidden, grad_out, weight, alive):
    early = lax.ppermute(hidden, "tp", [(t, t + 2) for t in (9, 11, 13)] + [(t, t - 2) for t in (2, 4, 6)])
    other = lax.ppermute(hidden, "tp", [(t, t ^ 1) for t in range(N_TP)])
    light = lax.ppermute(hidden, "tp", [(t, t - 1) for t in (10, 12, 14)] + [(t, t + 1) for t in (1, 3, 5)])
    plan, late, middle = pl.pallas_call(
        own_kernel,
        out_shape=[shape((16,), jnp.int32), shape((COMMON, TOK), BF16), shape((MID, TOK), BF16)],
        in_specs=[SMEM, VMEM],
        out_specs=[SMEM, VMEM, VMEM],
        compiler_params=params(24),
        name="own_window",
    )(alive.T, hidden)
    late = pl.pallas_call(
        late_kernel,
        out_shape=shape((COMMON, TOK), BF16),
        in_specs=[SMEM, VMEM, VMEM],
        out_specs=VMEM,
        compiler_params=params(24),
        name="late_window",
    )(plan, late, other)
    late = lax.ppermute(late, "tp", [(t, t + 2) for t in (6, 8, 10, 12)] + [(t, t - 2) for t in (3, 5, 7, 9)])
    middle = lax.ppermute(middle, "tp", [(7, 9), (8, 6)])
    step = 256
    tokens = block((step, SLOT), lambda i: (i, 0))
    grad_hidden, own = pl.pallas_call(
        hidden_kernel,
        grid=(TOK // step,),
        out_shape=[shape((TOK, SLOT), BF16), shape((COMMON, TOK), BF16)],
        in_specs=[SMEM, block((step, D), lambda i: (i, 0)), block((SLOT, D), lambda i: (0, 0)), tokens, tokens],
        out_specs=[tokens, block((COMMON, step), lambda i: (0, i))],
        scratch_shapes=[pltpu.VMEM((2, COMMON, SLOT), BF16)],
        compiler_params=params(50),
        cost_estimate=pl.CostEstimate(flops=2 * TOK * SLOT * (D + 2 * COMMON), bytes_accessed=16 << 20, transcendentals=0),
        name="hidden_grad",
    )(plan, grad_out, weight[0], hidden, other)
    own = pl.pallas_call(
        merge_kernel,
        out_shape=shape((COMMON, TOK), BF16),
        in_specs=[SMEM, VMEM, VMEM, VMEM, VMEM],
        out_specs=VMEM,
        compiler_params=params(24),
        name="merge",
    )(plan, middle, light, early, own)
    payload = pl.pallas_call(
        partial_kernel,
        out_shape=shape((NEAR, FAR * ROWS + PAD, 128), I16),
        in_specs=[VMEM] * 3,
        out_specs=VMEM,
        scratch_shapes=[pltpu.VMEM((COMMON, TOK), BF16), pltpu.VMEM((NEAR, FAR * ROWS, 128), F32)],
        compiler_params=params(32),
        name="partial",
    )(grad_out, own, late)
    payload = lax.all_to_all(
        payload, "rep", 0, 0, axis_index_groups=[[f * NEAR + n for n in range(NEAR)] for f in range(FAR)]
    )
    payload = pl.pallas_call(
        middle_kernel,
        out_shape=shape((FAR, ROWS + PAD, 128), I16),
        in_specs=[VMEM],
        out_specs=VMEM,
        scratch_shapes=[pltpu.VMEM((ROWS, 128), F32)],
        compiler_params=params(16),
        name="middle",
    )(payload)
    payload = lax.all_to_all(
        payload, "rep", 0, 0, axis_index_groups=[[f * NEAR + n for f in range(FAR)] for n in range(NEAR)]
    )
    grad_weight_t = pl.pallas_call(
        final_kernel,
        out_shape=shape((64, COMMON), F32),
        in_specs=[VMEM],
        out_specs=VMEM,
        scratch_shapes=[pltpu.VMEM((256, 128), F32)],
        compiler_params=params(16),
        name="final",
    )(payload)
    return grad_hidden, grad_weight_t.T


def solution(mesh):
    return jax.shard_map(
        local,
        mesh=mesh,
        in_specs=(P("rep", "tp"), P("rep", None), P("rep", "tp", None), P()),
        out_specs=(P("rep", "tp"), P("tp", "rep")),
        check_vma=False,
    )
```

```python
import functools

import jax
import jax.numpy as jnp
from jax import lax
from jax.experimental import pallas as pl
from jax.experimental.pallas import tpu as pltpu
from jax.sharding import PartitionSpec as P

FF = 7168
TOK, D, SLOT, COMMON = 1024, 2048, 512, 448
N_REP, N_TP = 32, 16
NEAR, FAR = 8, 4
ROWS = 224
GROUPS = ((0, 64), (64, 64), (128, 64), (192, 32))
UNITS = ((0, 0, 128), (128, 256, 96), (224, 128, 128), (352, 352, 96))
PAD = 16
LOG_LEVELS = 14.999
MID = 64
WIDTH, LIMIT, LATE_OWN, LATE_OTHER, LOCAL_OWN, LOCAL_OTHER, EARLY, LIGHT, MIDDLE, ODD, HAS_EARLY, HAS_LIGHT = range(12)
FACTOR = float(N_REP * TOK) ** -0.5
F32, BF16, I16 = jnp.float32, jnp.bfloat16, jnp.int16
VMEM = pl.BlockSpec(memory_space=pltpu.VMEM)
SMEM = pl.BlockSpec(memory_space=pltpu.SMEM)


def own_kernel(alive, own, plan, out, middle):
    replica, me = lax.axis_index("rep"), lax.axis_index("tp")
    live = jnp.int32(0)
    for t in range(N_TP):
        live += alive[t, replica]
    width = lax.div(jnp.int32(FF), live)

    def shift(device, slot):
        rank = jnp.int32(0)
        for t in range(N_TP):
            rank += jnp.where(t < device, alive[t, replica], 0)
        return jnp.where(alive[device, replica] == 1, slot * COMMON - rank * width, 4 * FF)

    other = me ^ 1
    back = even_odd(me, -2, 2)
    away = even_odd(me, 2, -2)
    plan[WIDTH] = width
    plan[LIMIT] = jnp.where(alive[me, replica] == 1, width, 0)
    plan[LATE_OWN] = shift(me, away)
    plan[LATE_OTHER] = shift(other, away)
    plan[LOCAL_OWN] = shift(me, me)
    plan[LOCAL_OTHER] = shift(other, me)
    plan[EARLY] = shift(jnp.clip(away, 0, N_TP - 1), me)
    plan[LIGHT] = shift(jnp.clip(even_odd(me, -1, 1), 0, N_TP - 1), me)
    plan[MIDDLE] = shift(me, back) + jnp.where(me % 2 == 0, COMMON - MID, 0)
    plan[ODD] = me % 2
    outer = jnp.where(me % 2 == 1, me, N_TP - 1 - me)
    plan[HAS_EARLY] = jnp.where(outer >= 11, 1, 0)
    plan[HAS_LIGHT] = jnp.where((outer >= 9) & (outer <= 13), 1, 0)
    late = selection(width, plan[LATE_OWN])
    small = selection(width, plan[MIDDLE], MID)
    for i in range(0, TOK, 256):
        out[:, i : i + 256] = across(late, own[i : i + 256]).astype(BF16)
        middle[:, i : i + 256] = across(small, own[i : i + 256]).astype(BF16)


def selection(width, shift, wanted=COMMON):
    ahead = lax.broadcasted_iota(jnp.int32, (wanted, SLOT), 1) - lax.broadcasted_iota(jnp.int32, (wanted, SLOT), 0)
    cols = lax.broadcasted_iota(jnp.int32, (wanted, SLOT), 1)
    return ((ahead == shift) & (cols < width)).astype(F32).astype(BF16)


def across(a, b):
    return lax.dot_general(a, b, (((1,), (1,)), ((), ())), preferred_element_type=F32)


def even_odd(me, even, odd):
    return me + jnp.where(me % 2 == 0, even, odd)


def late_kernel(plan, own, other, out):
    late = selection(plan[WIDTH], plan[LATE_OTHER])
    for i in range(0, TOK, 256):
        out[:, i : i + 256] = own[:, i : i + 256] + across(late, other[i : i + 256]).astype(BF16)


def merge_kernel(plan, middle, light, early, local, out):
    out[...] = local[...]
    for flag, shift, block in ((HAS_EARLY, EARLY, early), (HAS_LIGHT, LIGHT, light)):

        @pl.when(plan[flag] == 1)
        def _():
            out[...] = out[...] + across(selection(plan[WIDTH], plan[shift]), block[...]).astype(BF16)

    @pl.when(plan[ODD] == 1)
    def _():
        out[:MID] = out[:MID] + middle[...]

    @pl.when(plan[ODD] == 0)
    def _():
        out[COMMON - MID :] = out[COMMON - MID :] + middle[...]


def hidden_kernel(plan, grad, weight, own, other, grad_hidden, local, select):
    @pl.when(pl.program_id(0) == 0)
    def _():
        select[0] = selection(plan[WIDTH], plan[LOCAL_OWN])
        select[1] = selection(plan[WIDTH], plan[LOCAL_OTHER])

    block = grad[...]
    product = across(block, weight[...])
    cols = lax.broadcasted_iota(jnp.int32, product.shape, 1)
    grad_hidden[...] = jnp.where(cols < plan[LIMIT], product, 0.0).astype(BF16)
    local[...] = (across(select[0], own[...]) + across(select[1], other[...])).astype(BF16)


def steps_of(most):
    return jnp.ceil(256.0 * (jnp.log2(jnp.maximum(most, 1e-30)) - LOG_LEVELS))


def coded(value, inverse):
    return jnp.round(value * inverse).astype(jnp.int32).astype(I16)


def low_lanes(rows, below):
    return lax.broadcasted_iota(jnp.int32, (rows, 128), 1) < below


def fold(top, bottom):
    low = low_lanes(ROWS, 64)
    return jnp.where(low, top, pltpu.roll(bottom, 64, 1)), jnp.where(low, pltpu.roll(top, 64, 1), bottom)


def tallest(value):
    return jnp.max(jnp.abs(value).reshape(value.shape[0] // 8, 8, 128), axis=0)


def write_code(out, index, blocks, folded, most):
    steps = [steps_of(jnp.max(m, axis=0, keepdims=True)) for m in most]
    inverse = [jnp.exp2(step * (-1.0 / 256.0)) for step in steps]
    for block in range(blocks):
        for (row, rows), inv in zip(GROUPS, inverse):
            r = block * ROWS + row
            out[index, r : r + rows] = coded(folded(r, rows), inv)
    head = jnp.concatenate(steps + [jnp.zeros((PAD - len(steps), 128), F32)], axis=0)
    out[index, blocks * ROWS :] = head.astype(jnp.int32).astype(I16)


def read_steps(got, index, blocks):
    head = got[index, blocks * ROWS :].astype(jnp.int32).astype(F32)
    return jnp.exp2(head * (1.0 / 256.0))


def read_sum(got, sources, steps, r, rows, group):
    value = None
    for k in range(sources):
        term = got[k, r : r + rows].astype(jnp.int32).astype(F32) * steps[k][group : group + 1]
        value = term if value is None else value + term
    return value


def partial_kernel(grad, local, late, out, common, folded):
    for to, first, count in UNITS:
        common[to : to + count] = local[first : first + count] + late[first : first + count]
    wide = NEAR // 2 * 64
    for half in range(2):
        most = [[None] * len(GROUPS) for _ in range(NEAR)]
        for far in range(FAR):
            f = (far * 2 + half) * wide
            got = jnp.dot(common[...], grad[:, f : f + wide], preferred_element_type=F32)
            for c in range(0, wide, 128):
                near = half * (NEAR // 2) + c // 64
                for n, part in enumerate(fold(got[:ROWS, c : c + 128], got[ROWS:, c : c + 128]), near):
                    folded[n, far * ROWS : far * ROWS + ROWS] = part
                    for g, (row, rows) in enumerate(GROUPS):
                        big = tallest(part[row : row + rows])
                        most[n][g] = big if far == 0 else jnp.maximum(most[n][g], big)
        for n in range(half * (NEAR // 2), (half + 1) * (NEAR // 2)):
            write_code(out, n, FAR, lambda r, rows: folded[n, r : r + rows], most[n])


def middle_kernel(got, out, folded):
    steps = [read_steps(got, k, FAR) for k in range(NEAR)]
    for far in range(FAR):
        most = []
        for g, (row, rows) in enumerate(GROUPS):
            value = read_sum(got, NEAR, steps, far * ROWS + row, rows, g)
            folded[row : row + rows] = value
            most.append(tallest(value))
        write_code(out, far, 1, lambda r, rows: folded[r : r + rows], most)


def final_kernel(got, out, total):
    steps = [read_steps(got, k, 1) * FACTOR for k in range(FAR)]
    for g, (row, rows) in enumerate(GROUPS):
        total[row : row + rows] = read_sum(got, FAR, steps, row, rows, g)
    total[ROWS:] = jnp.zeros((256 - ROWS, 128), F32)
    turned = total[...].T
    out[:, :128] = turned[:64, :128]
    out[:, 128:256] = turned[64:, :128]
    rest = pltpu.roll(turned[64:, 128:], 96, 1)
    out[:, 256:384] = jnp.where(low_lanes(64, 96), turned[:64, 128:], rest)
    out[:, 384:] = rest[:, :64]


def shape(dims, kind):
    return jax.ShapeDtypeStruct(dims, kind)


def params(mib):
    return pltpu.CompilerParams(vmem_limit_bytes=mib << 20)


def block(dims, index):
    return pl.BlockSpec(dims, index)


def local(hidden, grad_out, weight, alive):
    early = lax.ppermute(hidden, "tp", [(t, t + 2) for t in (9, 11, 13)] + [(t, t - 2) for t in (2, 4, 6)])
    other = lax.ppermute(hidden, "tp", [(t, t ^ 1) for t in range(N_TP)])
    light = lax.ppermute(hidden, "tp", [(t, t - 1) for t in (10, 12, 14)] + [(t, t + 1) for t in (1, 3, 5)])
    plan, late, middle = pl.pallas_call(
        own_kernel,
        out_shape=[shape((16,), jnp.int32), shape((COMMON, TOK), BF16), shape((MID, TOK), BF16)],
        in_specs=[SMEM, VMEM],
        out_specs=[SMEM, VMEM, VMEM],
        compiler_params=params(24),
        name="own_window",
    )(alive.T, hidden)
    late = pl.pallas_call(
        late_kernel,
        out_shape=shape((COMMON, TOK), BF16),
        in_specs=[SMEM, VMEM, VMEM],
        out_specs=VMEM,
        compiler_params=params(24),
        name="late_window",
    )(plan, late, other)
    late = lax.ppermute(late, "tp", [(t, t + 2) for t in (6, 8, 10, 12)] + [(t, t - 2) for t in (3, 5, 7, 9)])
    middle = lax.ppermute(middle, "tp", [(7, 9), (8, 6)])
    step = 256
    tokens = block((step, SLOT), lambda i: (i, 0))
    grad_hidden, own = pl.pallas_call(
        hidden_kernel,
        grid=(TOK // step,),
        out_shape=[shape((TOK, SLOT), BF16), shape((COMMON, TOK), BF16)],
        in_specs=[SMEM, block((step, D), lambda i: (i, 0)), block((SLOT, D), lambda i: (0, 0)), tokens, tokens],
        out_specs=[tokens, block((COMMON, step), lambda i: (0, i))],
        scratch_shapes=[pltpu.VMEM((2, COMMON, SLOT), BF16)],
        compiler_params=params(50),
        cost_estimate=pl.CostEstimate(flops=2 * TOK * SLOT * (D + 2 * COMMON), bytes_accessed=16 << 20, transcendentals=0),
        name="hidden_grad",
    )(plan, grad_out, weight[0], hidden, other)
    own = pl.pallas_call(
        merge_kernel,
        out_shape=shape((COMMON, TOK), BF16),
        in_specs=[SMEM, VMEM, VMEM, VMEM, VMEM],
        out_specs=VMEM,
        compiler_params=params(24),
        name="merge",
    )(plan, middle, light, early, own)
    payload = pl.pallas_call(
        partial_kernel,
        out_shape=shape((NEAR, FAR * ROWS + PAD, 128), I16),
        in_specs=[VMEM] * 3,
        out_specs=VMEM,
        scratch_shapes=[pltpu.VMEM((COMMON, TOK), BF16), pltpu.VMEM((NEAR, FAR * ROWS, 128), F32)],
        compiler_params=params(32),
        name="partial",
    )(grad_out, own, late)
    payload = lax.all_to_all(
        payload, "rep", 0, 0, axis_index_groups=[[f * NEAR + n for n in range(NEAR)] for f in range(FAR)]
    )
    payload = pl.pallas_call(
        middle_kernel,
        out_shape=shape((FAR, ROWS + PAD, 128), I16),
        in_specs=[VMEM],
        out_specs=VMEM,
        scratch_shapes=[pltpu.VMEM((ROWS, 128), F32)],
        compiler_params=params(16),
        name="middle",
    )(payload)
    payload = lax.all_to_all(
        payload, "rep", 0, 0, axis_index_groups=[[f * NEAR + n for f in range(FAR)] for n in range(NEAR)]
    )
    grad_weight_t = pl.pallas_call(
        final_kernel,
        out_shape=shape((64, COMMON), F32),
        in_specs=[VMEM],
        out_specs=VMEM,
        scratch_shapes=[pltpu.VMEM((256, 128), F32)],
        compiler_params=params(16),
        name="final",
    )(payload)
    return grad_hidden, grad_weight_t.T


def solution(mesh):
    return jax.shard_map(
        local,
        mesh=mesh,
        in_specs=(P("rep", "tp"), P("rep", None), P("rep", "tp", None), P()),
        out_specs=(P("rep", "tp"), P("tp", "rep")),
        check_vma=False,
    )
```

```python
import functools

import jax
import jax.numpy as jnp
from jax import lax
from jax.experimental import pallas as pl
from jax.experimental.pallas import tpu as pltpu
from jax.sharding import PartitionSpec as P

FF = 7168
TOK, D, SLOT, COMMON = 1024, 2048, 512, 448
N_REP, N_TP = 32, 16
NEAR, FAR = 8, 4
ROWS = 224
GROUPS = ((0, 64), (64, 64), (128, 64), (192, 32))
UNITS = ((0, 0, 128), (128, 256, 96), (224, 128, 128), (352, 352, 96))
PAD = 16
LOG_LEVELS = 14.999
MID = 64
WIDTH, LIMIT, LATE_OWN, LATE_OTHER, LOCAL_OWN, LOCAL_OTHER, EARLY, LIGHT, MIDDLE, ODD, HAS_EARLY, HAS_LIGHT = range(12)
FACTOR = float(N_REP * TOK) ** -0.5
F32, BF16, I16 = jnp.float32, jnp.bfloat16, jnp.int16
VMEM = pl.BlockSpec(memory_space=pltpu.VMEM)
SMEM = pl.BlockSpec(memory_space=pltpu.SMEM)


def own_kernel(alive, own, plan, out, middle):
    replica, me = lax.axis_index("rep"), lax.axis_index("tp")
    live = jnp.int32(0)
    for t in range(N_TP):
        live += alive[t, replica]
    width = lax.div(jnp.int32(FF), live)

    def shift(device, slot):
        rank = jnp.int32(0)
        for t in range(N_TP):
            rank += jnp.where(t < device, alive[t, replica], 0)
        return jnp.where(alive[device, replica] == 1, slot * COMMON - rank * width, 4 * FF)

    other = me ^ 1
    back = even_odd(me, -2, 2)
    away = even_odd(me, 2, -2)
    plan[WIDTH] = width
    plan[LIMIT] = jnp.where(alive[me, replica] == 1, width, 0)
    plan[LATE_OWN] = shift(me, away)
    plan[LATE_OTHER] = shift(other, away)
    plan[LOCAL_OWN] = shift(me, me)
    plan[LOCAL_OTHER] = shift(other, me)
    plan[EARLY] = shift(jnp.clip(away, 0, N_TP - 1), me)
    plan[LIGHT] = shift(jnp.clip(even_odd(me, -1, 1), 0, N_TP - 1), me)
    plan[MIDDLE] = shift(me, back) + jnp.where(me % 2 == 0, COMMON - MID, 0)
    plan[ODD] = me % 2
    outer = jnp.where(me % 2 == 1, me, N_TP - 1 - me)
    plan[HAS_EARLY] = jnp.where(outer >= 11, 1, 0)
    plan[HAS_LIGHT] = jnp.where((outer >= 9) & (outer <= 13), 1, 0)
    late = selection(width, plan[LATE_OWN])
    small = selection(width, plan[MIDDLE], MID)
    for i in range(0, TOK, 512):
        out[:, i : i + 512] = across(late, own[i : i + 512]).astype(BF16)
        middle[:, i : i + 512] = across(small, own[i : i + 512]).astype(BF16)


def selection(width, shift, wanted=COMMON):
    ahead = lax.broadcasted_iota(jnp.int32, (wanted, SLOT), 1) - lax.broadcasted_iota(jnp.int32, (wanted, SLOT), 0)
    cols = lax.broadcasted_iota(jnp.int32, (wanted, SLOT), 1)
    return ((ahead == shift) & (cols < width)).astype(F32).astype(BF16)


def across(a, b):
    return lax.dot_general(a, b, (((1,), (1,)), ((), ())), preferred_element_type=F32)


def even_odd(me, even, odd):
    return me + jnp.where(me % 2 == 0, even, odd)


def late_kernel(plan, own, other, out):
    late = selection(plan[WIDTH], plan[LATE_OTHER])
    for i in range(0, TOK, 512):
        out[:, i : i + 512] = own[:, i : i + 512] + across(late, other[i : i + 512]).astype(BF16)


def merge_kernel(plan, middle, light, early, local, out):
    out[...] = local[...]
    for flag, shift, block in ((HAS_EARLY, EARLY, early), (HAS_LIGHT, LIGHT, light)):

        @pl.when(plan[flag] == 1)
        def _():
            out[...] = out[...] + across(selection(plan[WIDTH], plan[shift]), block[...]).astype(BF16)

    @pl.when(plan[ODD] == 1)
    def _():
        out[:MID] = out[:MID] + middle[...]

    @pl.when(plan[ODD] == 0)
    def _():
        out[COMMON - MID :] = out[COMMON - MID :] + middle[...]


def hidden_kernel(plan, grad, weight, own, other, grad_hidden, local, select):
    @pl.when(pl.program_id(0) == 0)
    def _():
        select[0] = selection(plan[WIDTH], plan[LOCAL_OWN])
        select[1] = selection(plan[WIDTH], plan[LOCAL_OTHER])

    block = grad[...]
    product = across(block, weight[...])
    cols = lax.broadcasted_iota(jnp.int32, product.shape, 1)
    grad_hidden[...] = jnp.where(cols < plan[LIMIT], product, 0.0).astype(BF16)
    local[...] = (across(select[0], own[...]) + across(select[1], other[...])).astype(BF16)


def steps_of(most):
    return jnp.ceil(256.0 * (jnp.log2(jnp.maximum(most, 1e-30)) - LOG_LEVELS))


def coded(value, inverse):
    return jnp.round(value * inverse).astype(jnp.int32).astype(I16)


def low_lanes(rows, below):
    return lax.broadcasted_iota(jnp.int32, (rows, 128), 1) < below


def fold(top, bottom):
    low = low_lanes(ROWS, 64)
    return jnp.where(low, top, pltpu.roll(bottom, 64, 1)), jnp.where(low, pltpu.roll(top, 64, 1), bottom)


def tallest(value):
    return jnp.max(jnp.abs(value).reshape(value.shape[0] // 8, 8, 128), axis=0)


def write_code(out, index, blocks, folded, most):
    steps = [steps_of(jnp.max(m, axis=0, keepdims=True)) for m in most]
    inverse = [jnp.exp2(step * (-1.0 / 256.0)) for step in steps]
    for block in range(blocks):
        for (row, rows), inv in zip(GROUPS, inverse):
            r = block * ROWS + row
            out[index, r : r + rows] = coded(folded(r, rows), inv)
    head = jnp.concatenate(steps + [jnp.zeros((PAD - len(steps), 128), F32)], axis=0)
    out[index, blocks * ROWS :] = head.astype(jnp.int32).astype(I16)


def read_steps(got, index, blocks):
    head = got[index, blocks * ROWS :].astype(jnp.int32).astype(F32)
    return jnp.exp2(head * (1.0 / 256.0))


def read_sum(got, sources, steps, r, rows, group):
    value = None
    for k in range(sources):
        term = got[k, r : r + rows].astype(jnp.int32).astype(F32) * steps[k][group : group + 1]
        value = term if value is None else value + term
    return value


def partial_kernel(grad, local, late, out, common, folded):
    for to, first, count in UNITS:
        common[to : to + count] = local[first : first + count] + late[first : first + count]
    wide = NEAR // 2 * 64
    for half in range(2):
        most = [[None] * len(GROUPS) for _ in range(NEAR)]
        for far in range(FAR):
            f = (far * 2 + half) * wide
            got = jnp.dot(common[...], grad[:, f : f + wide], preferred_element_type=F32)
            for c in range(0, wide, 128):
                near = half * (NEAR // 2) + c // 64
                for n, part in enumerate(fold(got[:ROWS, c : c + 128], got[ROWS:, c : c + 128]), near):
                    folded[n, far * ROWS : far * ROWS + ROWS] = part
                    for g, (row, rows) in enumerate(GROUPS):
                        big = tallest(part[row : row + rows])
                        most[n][g] = big if far == 0 else jnp.maximum(most[n][g], big)
        for n in range(half * (NEAR // 2), (half + 1) * (NEAR // 2)):
            write_code(out, n, FAR, lambda r, rows: folded[n, r : r + rows], most[n])


def middle_kernel(got, out, folded):
    steps = [read_steps(got, k, FAR) for k in range(NEAR)]
    for far in range(FAR):
        most = []
        for g, (row, rows) in enumerate(GROUPS):
            value = read_sum(got, NEAR, steps, far * ROWS + row, rows, g)
            folded[row : row + rows] = value
            most.append(tallest(value))
        write_code(out, far, 1, lambda r, rows: folded[r : r + rows], most)


def final_kernel(got, out, total):
    steps = [read_steps(got, k, 1) * FACTOR for k in range(FAR)]
    for g, (row, rows) in enumerate(GROUPS):
        total[row : row + rows] = read_sum(got, FAR, steps, row, rows, g)
    total[ROWS:] = jnp.zeros((256 - ROWS, 128), F32)
    turned = total[...].T
    out[:, :128] = turned[:64, :128]
    out[:, 128:256] = turned[64:, :128]
    rest = pltpu.roll(turned[64:, 128:], 96, 1)
    out[:, 256:384] = jnp.where(low_lanes(64, 96), turned[:64, 128:], rest)
    out[:, 384:] = rest[:, :64]


def shape(dims, kind):
    return jax.ShapeDtypeStruct(dims, kind)


def params(mib):
    return pltpu.CompilerParams(vmem_limit_bytes=mib << 20)


def block(dims, index):
    return pl.BlockSpec(dims, index)


def local(hidden, grad_out, weight, alive):
    early = lax.ppermute(hidden, "tp", [(t, t + 2) for t in (9, 11, 13)] + [(t, t - 2) for t in (2, 4, 6)])
    other = lax.ppermute(hidden, "tp", [(t, t ^ 1) for t in range(N_TP)])
    light = lax.ppermute(hidden, "tp", [(t, t - 1) for t in (10, 12, 14)] + [(t, t + 1) for t in (1, 3, 5)])
    plan, late, middle = pl.pallas_call(
        own_kernel,
        out_shape=[shape((16,), jnp.int32), shape((COMMON, TOK), BF16), shape((MID, TOK), BF16)],
        in_specs=[SMEM, VMEM],
        out_specs=[SMEM, VMEM, VMEM],
        compiler_params=params(24),
        name="own_window",
    )(alive.T, hidden)
    late = pl.pallas_call(
        late_kernel,
        out_shape=shape((COMMON, TOK), BF16),
        in_specs=[SMEM, VMEM, VMEM],
        out_specs=VMEM,
        compiler_params=params(24),
        name="late_window",
    )(plan, late, other)
    late = lax.ppermute(late, "tp", [(t, t + 2) for t in (6, 8, 10, 12)] + [(t, t - 2) for t in (3, 5, 7, 9)])
    middle = lax.ppermute(middle, "tp", [(7, 9), (8, 6)])
    step = 256
    tokens = block((step, SLOT), lambda i: (i, 0))
    grad_hidden, own = pl.pallas_call(
        hidden_kernel,
        grid=(TOK // step,),
        out_shape=[shape((TOK, SLOT), BF16), shape((COMMON, TOK), BF16)],
        in_specs=[SMEM, block((step, D), lambda i: (i, 0)), block((SLOT, D), lambda i: (0, 0)), tokens, tokens],
        out_specs=[tokens, block((COMMON, step), lambda i: (0, i))],
        scratch_shapes=[pltpu.VMEM((2, COMMON, SLOT), BF16)],
        compiler_params=params(50),
        cost_estimate=pl.CostEstimate(flops=2 * TOK * SLOT * (D + 2 * COMMON), bytes_accessed=16 << 20, transcendentals=0),
        name="hidden_grad",
    )(plan, grad_out, weight[0], hidden, other)
    own = pl.pallas_call(
        merge_kernel,
        out_shape=shape((COMMON, TOK), BF16),
        in_specs=[SMEM, VMEM, VMEM, VMEM, VMEM],
        out_specs=VMEM,
        compiler_params=params(24),
        name="merge",
    )(plan, middle, light, early, own)
    payload = pl.pallas_call(
        partial_kernel,
        out_shape=shape((NEAR, FAR * ROWS + PAD, 128), I16),
        in_specs=[VMEM] * 3,
        out_specs=VMEM,
        scratch_shapes=[pltpu.VMEM((COMMON, TOK), BF16), pltpu.VMEM((NEAR, FAR * ROWS, 128), F32)],
        compiler_params=params(32),
        name="partial",
    )(grad_out, own, late)
    payload = lax.all_to_all(
        payload, "rep", 0, 0, axis_index_groups=[[f * NEAR + n for n in range(NEAR)] for f in range(FAR)]
    )
    payload = pl.pallas_call(
        middle_kernel,
        out_shape=shape((FAR, ROWS + PAD, 128), I16),
        in_specs=[VMEM],
        out_specs=VMEM,
        scratch_shapes=[pltpu.VMEM((ROWS, 128), F32)],
        compiler_params=params(16),
        name="middle",
    )(payload)
    payload = lax.all_to_all(
        payload, "rep", 0, 0, axis_index_groups=[[f * NEAR + n for f in range(FAR)] for n in range(NEAR)]
    )
    grad_weight_t = pl.pallas_call(
        final_kernel,
        out_shape=shape((64, COMMON), F32),
        in_specs=[VMEM],
        out_specs=VMEM,
        scratch_shapes=[pltpu.VMEM((256, 128), F32)],
        compiler_params=params(16),
        name="final",
    )(payload)
    return grad_hidden, grad_weight_t.T


def solution(mesh):
    return jax.shard_map(
        local,
        mesh=mesh,
        in_specs=(P("rep", "tp"), P("rep", None), P("rep", "tp", None), P()),
        out_specs=(P("rep", "tp"), P("tp", "rep")),
        check_vma=False,
    )
```
